1024 devices in a mesh: wide: 64 (over y, x, core), group: 16 (over z).
Axes of the slice: x: 4, y: 8, z: 16, core: 2. Of those that a mesh axis runs over, the one named last changes fastest.
Arguments:
- queries: bfloat16 [262144, 256], P(('wide', 'group')), may hold values from -100 to 100
- items: bfloat16 [262144, 256], P(('wide', 'group')), may hold values from -8 to 8
- cold_table: float32 [524288, 256], P(('wide', 'group')), may hold values from -6 to 6
- accum: float32 [524288, 256], P(('wide', 'group')), may hold values from 1e-09 to 1e-08
- send_rows: int32 [65536, 16], P(('wide', 'group')), may hold values from 0 to 511
- live_counts: int32 [1024, 64], P(('wide', 'group')), may hold values from 1 to 16, as said below
Outputs:
- query_grad: float32 [262144, 256], P(('wide', 'group'))
- item_grad: float32 [262144, 256], P(('wide', 'group'))
- new_table: float32 [524288, 256], P(('wide', 'group'))
The draws below stay inside these ranges and needn't reach their ends.
Inputs may be any that keep to these rules, and one draw needn't show every extreme that they name: `live_counts`: one owner index, drawn afresh, has all 16 slots live for every device.
All inputs are finite; a program needn't handle non-finite values.
Results may differ from the reference program's by a relative error of at most 0.00525.
Values may be sent and summed in bfloat16 or wider, within the bound.
A program may use at most 32 MiB of HBM per device.

```python
import math
import jax
import jax.numpy as jnp
from jax import lax

D = 256
Q_DEV = 256
CAP = 16
ROWS_DEV = 512
TOKENS = 262144
COLD = 524288
PLANS = 65536
N_WIDE = 64
N_GROUP = 16


def shared_parts(key):
    first = jax.random.fold_in(key, 0)
    half = N_GROUP // 2
    common = jax.random.normal(first, (N_WIDE, half, Q_DEV, D), jnp.float32)
    common = jnp.concatenate([common, common], axis=1).reshape(TOKENS, D)
    return common


def mix_weights():
    strong = min(0.92, (8.5 / D ** 0.5) ** 0.5)
    return (strong, (1.0 - strong * strong) ** 0.5)


def draw_items(key, part):
    common = shared_parts(key)
    key = jax.random.fold_in(key, 11)
    first = jax.random.fold_in(key, 0)
    own = jax.random.normal(first, (TOKENS, D), jnp.float32)
    strong, weak = mix_weights()
    values = strong * common + weak * own
    return jnp.clip(values, -6.0, 6.0).astype(jnp.bfloat16)


def draw_queries(key, part):
    common = shared_parts(key)
    key = jax.random.fold_in(key, 12)
    first = jax.random.fold_in(key, 0)
    own = jax.random.normal(first, (TOKENS, D), jnp.float32)
    strong, weak = mix_weights()
    return jnp.clip(strong * common + weak * own, -6.0, 6.0).astype(jnp.bfloat16)


def draw_live_counts(key, part):
    key = jax.random.fold_in(key, 5)
    first, second = jax.random.split(key)
    counts = jax.random.randint(first, (N_WIDE * N_GROUP, N_WIDE), 1, CAP + 1)
    full_owner = jax.random.randint(second, (), 0, N_WIDE)
    return jnp.where(jnp.arange(N_WIDE)[None, :] == full_owner, CAP, counts).astype(jnp.int32)


def set_ends(values, own_key, smallest, top_value):
    longest = values.shape.index(max(values.shape))
    spots = []
    for shift in (0, 1):
        where = [jax.random.randint(jax.random.fold_in(own_key, axis), (), 0, length) for axis, length in enumerate(values.shape)]
        where[longest] = (where[longest] + shift) % values.shape[longest]
        spots.append(tuple(where))
    return values.at[spots[0]].set(smallest).at[spots[1]].set(top_value)


def steps_of(rng, shape, pieces, smallest, largest):
    level = 1.0
    for axis_at, shards_of in pieces:
        steps = jax.random.uniform(jax.random.fold_in(jax.random.fold_in(rng, 6), axis_at), (shards_of,), jnp.float32, smallest / len(pieces), largest / len(pieces))
        level = level * jnp.repeat(jnp.exp(steps), shape[axis_at] // shards_of).reshape((-1,) + (1,) * (len(shape) - 1 - axis_at))
    return level


def noise(rng, dims, scale, bound, shards=(), dtype=jnp.bfloat16):
    array = jax.random.normal(rng, dims, jnp.float32) * scale
    if len(shards) > 0:
        array = steps_of(rng, dims, shards, -0.22, 0.18) * array
    return jnp.clip(array, min=-bound, max=bound).astype(dtype)


def setup_inputs(seed: int = 0) -> dict:
    streams_of = jax.random.split(jax.random.key(seed), 7)
    return {
        "queries": draw_queries(jax.random.fold_in(streams_of[6], 71), 0),
        "items": draw_items(jax.random.fold_in(streams_of[6], 71), 0),
        "cold_table": noise(streams_of[2], (COLD, D), 1.0, 6.0, ((0, 1024),), jnp.float32),
        "accum": jnp.clip(jnp.exp(math.log(9.99999993922529e-09) - 2.3025851 * jax.random.uniform(streams_of[3], (COLD, D), jnp.float32) ** steps_of(streams_of[3], (COLD, D), ((0, 1024),), -0.2, 0.2)), 9.999999717180685e-10, 9.99999993922529e-09),
        "send_rows": set_ends(jax.random.randint(streams_of[4], (PLANS, CAP), 0, ROWS_DEV), jax.random.fold_in(streams_of[4], 1), 0, ROWS_DEV - 1).astype(jnp.int32),
        "live_counts": draw_live_counts(jax.random.fold_in(streams_of[6], 71), 0),
    }


def reference(queries, items, cold_table, accum, send_rows, live_counts):
    scale = D ** (-0.5)
    line = N_GROUP * Q_DEV
    query4 = queries.reshape(N_WIDE, N_GROUP, Q_DEV, D)
    item3 = items.reshape(N_WIDE, line, D)
    table4 = cold_table.reshape(N_WIDE, N_GROUP, ROWS_DEV, D)
    send4 = send_rows.reshape(N_WIDE, N_GROUP, N_WIDE, CAP)
    counts3 = live_counts.reshape(N_WIDE, N_GROUP, N_WIDE)
    target = jnp.arange(N_GROUP)[:, None] * Q_DEV + jnp.arange(Q_DEV)[None, :]
    owner_ids = jnp.arange(N_WIDE)[:, None, None]
    group_ids = jnp.arange(N_GROUP)[None, :, None]
    slot_ids = jnp.arange(CAP)
    highest = lax.Precision.HIGHEST

    def one_line(grads, w):
        query = query4[w].astype(jnp.float32)
        keys = item3[w].astype(jnp.float32)
        picked = send4[:, :, w, :]
        cold = table4[owner_ids, group_ids, picked].astype(jnp.bfloat16)
        cold = lax.optimization_barrier(cold).astype(jnp.float32)
        cold = jnp.transpose(cold, (1, 0, 2, 3)).reshape(N_GROUP, N_WIDE * CAP, D)
        live = (slot_ids[None, None, :] < counts3[w][:, :, None]).reshape(N_GROUP, N_WIDE * CAP)
        s_in = jnp.einsum('gqd,kd->gqk', query, keys, precision=highest) * scale
        s_cold = jnp.einsum('gqd,gkd->gqk', query, cold, precision=highest) * scale
        s_cold = jnp.where(live[:, None, :], s_cold, -jnp.inf)
        top = jnp.maximum(lax.optimization_barrier(jnp.max(s_in, axis=-1)), lax.optimization_barrier(jnp.max(s_cold, axis=-1)))
        total = lax.optimization_barrier(jnp.sum(jnp.exp(s_in - top[..., None]), axis=-1)) + lax.optimization_barrier(jnp.sum(jnp.exp(s_cold - top[..., None]), axis=-1))
        lse = top + jnp.log(total)
        onehot = (jnp.arange(line)[None, None, :] == target[:, :, None]).astype(jnp.float32)
        d_in = (jnp.exp(s_in - lse[..., None]) - onehot).astype(jnp.bfloat16)
        d_cold = jnp.exp(s_cold - lse[..., None]).astype(jnp.bfloat16)
        d_in = lax.optimization_barrier(d_in).astype(jnp.float32)
        d_cold = lax.optimization_barrier(d_cold).astype(jnp.float32)
        query_grad = (jnp.einsum('gqk,kd->gqd', d_in, keys, precision=highest) + jnp.einsum('gqk,gkd->gqd', d_cold, cold, precision=highest)) * scale
        item_grad = jnp.einsum('gqk,gqd->kd', d_in, query, precision=highest) * scale
        slot_grads = jnp.einsum('gqk,gqd->gkd', d_cold, query, precision=highest) * scale
        slot_grads = jnp.transpose(slot_grads.reshape(N_GROUP, N_WIDE, CAP, D), (1, 0, 2, 3))
        grads = grads.at[owner_ids, group_ids, picked].add(slot_grads)
        return (grads, (query_grad.reshape(line, D), item_grad))
    start = jnp.zeros((N_WIDE, N_GROUP, ROWS_DEV, D), jnp.float32)
    grads, outs = lax.scan(one_line, start, jnp.arange(N_WIDE))
    query_grad = outs[0].reshape(TOKENS, D)
    item_grad = outs[1].reshape(TOKENS, D)
    grads = grads.reshape(COLD, D)
    new_accum = accum + grads * grads
    new_table = cold_table - 0.5 * grads / jnp.sqrt(new_accum)
    return (query_grad, item_grad, new_table)
```

```python
import functools

import jax
import jax.numpy as jnp
from jax import lax
from jax.experimental import pallas as pl
from jax.experimental.pallas import tpu as pltpu
from jax.sharding import PartitionSpec as P

MESH = pl.DeviceIdType.MESH
NT = (((1,), (1,)), ((), ()))
TN = (((0,), (0,)), ((), ()))
F32 = jnp.float32
BF16 = jnp.bfloat16


def dot(a, b, dims=(((1,), (0,)), ((), ()))):
    return lax.dot_general(a, b, dims, preferred_element_type=F32)


def as_bf16(condition):
    return jnp.where(condition, 1.0, 0.0).astype(BF16)


def kernel(
    n_w,
    n_g,
    cap,
    queries,
    items,
    table_hbm,
    accum_hbm,
    send_rows,
    live_counts,
    query_grad,
    item_grad,
    new_table,
    keys,
    line_q,
    lse_all,
    s_in,
    s_cold,
    top8,
    sum8,
    table,
    accum,
    cold_out,
    cold_keys,
    slot_out,
    slot_back,
    query_t,
    load_sem,
    item_send,
    item_recv,
    q_send,
    q_recv,
    lse_send,
    lse_recv,
    wide_send,
    wide_recv,
):
    w, g = lax.axis_index("wide"), lax.axis_index("group")
    right, left = lax.rem(g + 1, n_g), lax.rem(g + n_g - 1, n_g)
    half = n_g // 2
    rows, depth = queries.shape
    chunk = rows // 2
    slots = n_w * cap
    table_rows = table.shape[0]
    scale = depth ** (-0.5)

    loads = [
        pltpu.make_async_copy(items, keys.at[0], load_sem.at[0]),
        pltpu.make_async_copy(queries, line_q.at[0], load_sem.at[1]),
        pltpu.make_async_copy(table_hbm, table, load_sem.at[2]),
        pltpu.make_async_copy(accum_hbm, accum, load_sem.at[3]),
    ]
    for load in loads:
        load.start()

    barrier = pltpu.get_barrier_semaphore()

    @pl.loop(1, n_g)
    def _(p):
        pl.semaphore_signal(
            barrier, inc=1, device_id=(w, lax.rem(g + p, n_g)), device_id_type=MESH
        )

    @pl.loop(1, n_w)
    def _(p):
        pl.semaphore_signal(
            barrier, inc=1, device_id=(lax.rem(w + p, n_w), g), device_id_type=MESH
        )

    def ring(buffer, send, recv, way, step, part):
        at = pl.ds(part * chunk, chunk)
        src, dst = (step - 1, step) if way == 0 else ((n_g + 1 - step) % n_g, n_g - step)
        return pltpu.make_async_remote_copy(
            src_ref=buffer.at[src, at],
            dst_ref=buffer.at[dst, at],
            send_sem=send.at[way, step, part],
            recv_sem=recv.at[way, step, part],
            device_id=(w, right if way == 0 else left),
            device_id_type=MESH,
        )

    def pieces(step):
        if isinstance(step, int) and step == half:
            return ((0, 0), (1, 1))
        return ((0, 0), (1, 0), (0, 1), (1, 1))

    def ring_start(buffer, send, recv, step):
        for way, part in pieces(step):
            ring(buffer, send, recv, way, step, part).start()

    def ring_pass(buffer, send, recv, step, last):
        for way, part in pieces(step):
            ring(buffer, send, recv, way, step, part).wait_recv()
            if not last or way == part:
                ring(buffer, send, recv, way, step + 1, part).start()

    def ring_end(buffer, send, recv):
        for way, part in pieces(half):
            ring(buffer, send, recv, way, half, part).wait_recv()

    def ring_drain(buffer, send, recv):
        @pl.loop(1, half)
        def _(step):
            for way, part in pieces(step):
                ring(buffer, send, recv, way, step, part).wait_send()

        for way, part in pieces(half):
            ring(buffer, send, recv, way, half, part).wait_send()

    item_ring = (keys, item_send, item_recv)
    query_ring = (line_q, q_send, q_recv)

    def wide_start(src, dst, k, peer):
        @pl.when(peer != w)
        def _():
            pltpu.make_async_remote_copy(
                src_ref=src.at[peer],
                dst_ref=dst.at[w],
                send_sem=wide_send.at[k],
                recv_sem=wide_recv.at[k],
                device_id=(peer, g),
                device_id_type=MESH,
            ).start()

        @pl.when(peer == w)
        def _():
            pltpu.make_async_copy(src.at[w], dst.at[w], wide_recv.at[k]).start()

    def wide_arrived(dst, k):
        pltpu.make_async_copy(dst, dst, wide_recv.at[k]).wait()

    def wide_drain(src, k):
        others = src.at[pl.ds(0, n_w - 1)]
        pltpu.make_async_copy(others, others, wide_send.at[k]).wait()

    owner = lax.broadcasted_iota(jnp.int32, (slots, n_w), 1)
    slot = lax.broadcasted_iota(jnp.int32, (slots, n_w), 0)
    spread = as_bf16(lax.div(slot, cap) == owner)
    picks = send_rows[...]
    high = (picks & ~15).astype(F32).astype(BF16)
    low = (picks & 15).astype(F32).astype(BF16)
    place = lax.broadcasted_iota(jnp.int32, (slots, cap), 1)
    slot = lax.broadcasted_iota(jnp.int32, (slots, cap), 0)
    mine = lax.rem(slot, cap) == place
    high = jnp.where(mine, dot(spread, high), 0.0).astype(BF16)
    low = jnp.where(mine, dot(spread, low), 0.0).astype(BF16)
    ones = jnp.ones((cap, table_rows), BF16)
    row_of = dot(high, ones) + dot(low, ones)
    row = lax.broadcasted_iota(jnp.int32, (slots, table_rows), 1).astype(F32)
    pick = as_bf16(row_of == row)
    loads[2].wait()
    fetched = dot(pick, table[...].astype(BF16)).astype(BF16)
    cold_out[...] = fetched.reshape(n_w, cap, depth)

    loads[0].wait()
    loads[1].wait()
    query_t[...] = jnp.transpose(line_q[0])

    pl.semaphore_wait(barrier, n_g - 1 + n_w - 1)
    ring_start(*item_ring, 1)

    @pl.loop(1, n_w + 1)
    def _(p):
        wide_start(cold_out, cold_keys, 0, lax.rem(w + p, n_w))

    def fold(s, first=False):
        s3 = s.reshape(s.shape[0] // 8, 8, s.shape[1])
        top = jnp.max(s3, axis=0)
        if first:
            top8[...] = top
            sum8[...] = jnp.sum(jnp.exp(s3 - top[None]), axis=0)
        else:
            before = top8[...]
            top = jnp.maximum(before, top)
            top8[...] = top
            sum8[...] = sum8[...] * jnp.exp(before - top) + jnp.sum(jnp.exp(s3 - top[None]), axis=0)

    def score(block, first=False):
        s = dot(keys[block], query_t[...]) * scale
        s_in[block] = s
        fold(s, first)

    score(0, first=True)

    cold_blocks = max(slots // 256, 1)
    cold_rows = slots // cold_blocks

    def score_cold(k):
        at = pl.ds(k * cold_rows, cold_rows)
        owner = lax.broadcasted_iota(jnp.int32, (cold_rows, n_w), 1)
        slot = lax.broadcasted_iota(jnp.int32, (cold_rows, n_w), 0) + k * cold_rows
        spread = as_bf16(lax.div(slot, cap) == owner)
        counts = jnp.broadcast_to(live_counts[...].astype(F32).astype(BF16), (rows, n_w))
        counts = dot(spread, counts, NT)
        place = lax.rem(lax.broadcasted_iota(jnp.int32, (cold_rows, rows), 0), cap).astype(F32)
        owners = pl.ds(k * (n_w // cold_blocks), n_w // cold_blocks)
        found = cold_keys[owners].reshape(cold_rows, depth)
        s = dot(found, query_t[...]) * scale
        s = jnp.where(place < counts, s, -jnp.inf)
        s_cold[at] = s
        fold(s)


    @pl.loop(1, half - 1)
    def _(step):
        ring_pass(*item_ring, step, False)
        score(step)
        score(n_g - step)

    ring_pass(*item_ring, half - 1, True)
    ring_start(*query_ring, 1)
    wide_arrived(cold_keys, 0)

    @pl.loop(0, cold_blocks)
    def _(k):
        score_cold(k)

    score(half - 1)
    if half > 1:
        score(half + 1)
    ring_end(*item_ring)
    score(half)

    top = jnp.max(top8[...], axis=0, keepdims=True)
    total = jnp.sum(sum8[...] * jnp.exp(top8[...] - top), axis=0, keepdims=True)
    lse_all[0] = top + jnp.log(total)

    def lse_copy(p):
        return pltpu.make_async_remote_copy(
            src_ref=lse_all.at[0],
            dst_ref=lse_all.at[p],
            send_sem=lse_send.at[p],
            recv_sem=lse_recv.at[p],
            device_id=(w, lax.rem(g + p, n_g)),
            device_id_type=MESH,
        )

    @pl.loop(1, n_g)
    def _(p):
        lse_copy(p).start()

    per = n_w // cold_blocks
    own_part = lax.div(w, per)

    @pl.loop(0, cold_blocks)
    def _(i):
        k = lax.rem(own_part + i, cold_blocks)
        at = pl.ds(pl.multiple_of(k * cold_rows, cold_rows), cold_rows)
        d = jnp.exp(s_cold[at] - lse_all[0]).astype(BF16)
        back = (dot(d, line_q[0]) * scale).astype(BF16)
        slot_out[pl.ds(k * per, per)] = back.reshape(per, cap, depth)

        @pl.loop(0, per)
        def _(j):
            wide_start(slot_out, slot_back, 1, k * per + lax.rem(w + j, per))

    ring_pass(*query_ring, 1, half == 2)

    d = jnp.exp(s_in[0] - lse_all[0])
    key = lax.broadcasted_iota(jnp.int32, d.shape, 0)
    query = lax.broadcasted_iota(jnp.int32, d.shape, 1)
    d = (d - jnp.where(key == query, 1.0, 0.0)).astype(BF16)
    query_grad[...] = dot(d, keys[0], TN)
    item_grad[...] = dot(d, line_q[0])

    def to_queries(block):
        d = jnp.exp(s_in[block] - lse_all[0]).astype(BF16)
        query_grad[...] += dot(d, keys[block], TN)

    def to_items(block):
        lse_copy(block).wait_recv()
        s = dot(keys[0], line_q[block], NT) * scale
        d = jnp.exp(s - lse_all[block]).astype(BF16)
        item_grad[...] += dot(d, line_q[block])

    @pl.loop(1, half - 1)
    def _(step):
        @pl.when(step > 1)
        def _():
            ring_pass(*query_ring, step, False)

        to_queries(step)
        to_queries(n_g - step)
        to_items(step)
        to_items(n_g - step)

    if half > 2:
        ring_pass(*query_ring, half - 1, True)
    to_queries(half - 1)
    to_queries(half)
    to_queries(half + 1)

    @pl.loop(0, cold_blocks)
    def _(k):
        d = jnp.exp(s_cold[pl.ds(k * cold_rows, cold_rows)] - lse_all[0]).astype(BF16)
        found = cold_keys[pl.ds(k * per, per)].reshape(cold_rows, depth)
        query_grad[...] += dot(d, found, TN)

    query_grad[...] = query_grad[...] * scale

    owner = lax.broadcasted_iota(jnp.int32, (n_w, slots), 0)
    slot = lax.broadcasted_iota(jnp.int32, (n_w, slots), 1)
    spread = as_bf16(lax.div(slot, cap) == owner)
    picks = send_rows[...]
    high = dot((picks & ~15).astype(F32).astype(BF16), spread, TN)
    low = dot((picks & 15).astype(F32).astype(BF16), spread, TN)
    place = lax.broadcasted_iota(jnp.int32, (cap, slots), 0)
    slot = lax.broadcasted_iota(jnp.int32, (cap, slots), 1)
    row_of = jnp.sum(
        jnp.where(lax.rem(slot, cap) == place, high + low, 0.0), axis=0, keepdims=True
    )
    row = lax.broadcasted_iota(jnp.int32, (table_rows, slots), 0).astype(F32)
    put = as_bf16(row_of == row)
    wide_arrived(slot_back, 1)
    loads[3].wait()
    grad = dot(put, slot_back[...].reshape(slots, depth))
    new_table[...] = table[...] - 0.5 * grad / jnp.sqrt(accum[...] + grad * grad)

    to_items(half - 1)
    to_items(half + 1)
    ring_end(*query_ring)
    to_items(half)
    item_grad[...] = item_grad[...] * scale

    wide_drain(cold_out, 0)
    wide_drain(slot_out, 1)

    @pl.loop(1, n_g)
    def _(p):
        lse_copy(p).wait_send()

    ring_drain(*item_ring)
    ring_drain(*query_ring)


def on_device(n_w, n_g, queries, items, cold_table, accum, send_rows, live_counts):
    rows, depth = queries.shape
    table_rows = cold_table.shape[0]
    cap = send_rows.shape[1]
    slots = n_w * cap
    half = n_g // 2
    vmem = pl.BlockSpec(memory_space=pltpu.VMEM)
    hbm = pl.BlockSpec(memory_space=pl.ANY)
    ring_sems = pltpu.SemaphoreType.DMA((2, half + 1, 2))
    return pl.pallas_call(
        functools.partial(kernel, n_w, n_g, cap),
        out_shape=(
            jax.ShapeDtypeStruct((rows, depth), F32),
            jax.ShapeDtypeStruct((rows, depth), F32),
            jax.ShapeDtypeStruct((table_rows, depth), F32),
        ),
        in_specs=[hbm, hbm, hbm, hbm, vmem, vmem],
        out_specs=(vmem, vmem, vmem),
        scratch_shapes=[
            pltpu.VMEM((n_g, rows, depth), BF16),
            pltpu.VMEM((n_g, rows, depth), BF16),
            pltpu.VMEM((n_g, 1, rows), F32),
            pltpu.VMEM((n_g, rows, rows), F32),
            pltpu.VMEM((slots, rows), F32),
            pltpu.VMEM((8, rows), F32),
            pltpu.VMEM((8, rows), F32),
            pltpu.VMEM((table_rows, depth), F32),
            pltpu.VMEM((table_rows, depth), F32),
            pltpu.VMEM((n_w, cap, depth), BF16),
            pltpu.VMEM((n_w, cap, depth), BF16),
            pltpu.VMEM((n_w, cap, depth), BF16),
            pltpu.VMEM((n_w, cap, depth), BF16),
            pltpu.VMEM((depth, rows), BF16),
            pltpu.SemaphoreType.DMA((4,)),
            ring_sems,
            ring_sems,
            ring_sems,
            ring_sems,
            pltpu.SemaphoreType.DMA((n_g,)),
            pltpu.SemaphoreType.DMA((n_g,)),
            pltpu.SemaphoreType.DMA((2,)),
            pltpu.SemaphoreType.DMA((2,)),
        ],
        compiler_params=pltpu.CompilerParams(
            collective_id=0, has_side_effects=True, vmem_limit_bytes=40 * 1024 * 1024
        ),
    )(queries, items, cold_table, accum, send_rows, live_counts)


def solution(mesh):
    spec = P(("wide", "group"), None)
    return jax.shard_map(
        functools.partial(on_device, mesh.shape["wide"], mesh.shape["group"]),
        mesh=mesh,
        in_specs=(spec,) * 6,
        out_specs=(spec,) * 3,
        check_vma=False,
    )
```

```python
import functools

import jax
import jax.numpy as jnp
from jax import lax
from jax.experimental import pallas as pl
from jax.experimental.pallas import tpu as pltpu
from jax.sharding import PartitionSpec as P

MESH = pl.DeviceIdType.MESH
NT = (((1,), (1,)), ((), ()))
TN = (((0,), (0,)), ((), ()))
F32 = jnp.float32
BF16 = jnp.bfloat16


def dot(a, b, dims=(((1,), (0,)), ((), ()))):
    return lax.dot_general(a, b, dims, preferred_element_type=F32)


def as_bf16(condition):
    return jnp.where(condition, 1.0, 0.0).astype(BF16)


def kernel(
    n_w,
    n_g,
    cap,
    queries,
    items,
    table_hbm,
    accum_hbm,
    send_rows,
    live_counts,
    query_grad_hbm,
    item_grad_hbm,
    new_table_hbm,
    query_grad,
    item_grad,
    new_table,
    keys,
    line_q,
    lse_all,
    s_in,
    s_back,
    s_cold,
    top8,
    sum8,
    table,
    accum,
    cold_out,
    cold_keys,
    slot_out,
    slot_back,
    query_t,
    put,
    load_sem,
    save_sem,
    ring_send,
    ring_recv,
    lse_send,
    lse_recv,
    wide_send,
    wide_recv,
):
    w, g = lax.axis_index("wide"), lax.axis_index("group")
    right, left = lax.rem(g + 1, n_g), lax.rem(g + n_g - 1, n_g)
    half = n_g // 2
    rows, depth = queries.shape
    chunk = rows // 2
    slots = n_w * cap
    table_rows = table.shape[0]
    scale = depth ** (-0.5)
    cold_blocks = max(slots // 256, 1)
    cold_rows = slots // cold_blocks

    loads = [
        pltpu.make_async_copy(items, keys.at[0], load_sem.at[0]),
        pltpu.make_async_copy(queries, line_q.at[0], load_sem.at[1]),
        pltpu.make_async_copy(table_hbm, table, load_sem.at[2]),
        pltpu.make_async_copy(accum_hbm, accum, load_sem.at[3]),
    ]
    for load in loads:
        load.start()

    saves = [
        pltpu.make_async_copy(query_grad, query_grad_hbm, save_sem.at[0]),
        pltpu.make_async_copy(item_grad, item_grad_hbm, save_sem.at[1]),
        pltpu.make_async_copy(new_table, new_table_hbm, save_sem.at[2]),
    ]

    barrier = pltpu.get_barrier_semaphore()

    @pl.loop(1, n_g)
    def _(p):
        pl.semaphore_signal(
            barrier, inc=1, device_id=(w, lax.rem(g + p, n_g)), device_id_type=MESH
        )

    @pl.loop(1, n_w)
    def _(p):
        pl.semaphore_signal(
            barrier, inc=1, device_id=(lax.rem(w + p, n_w), g), device_id_type=MESH
        )

    def ring(line, way, part, step):
        at = pl.ds(part * chunk, chunk)
        src, dst = (step - 1, step) if way == 0 else (lax.rem(n_g + 1 - step, n_g), n_g - step)
        buffer = line_q if line else keys
        return pltpu.make_async_remote_copy(
            src_ref=buffer.at[src, at],
            dst_ref=buffer.at[dst, at],
            send_sem=ring_send.at[line, way, part, step],
            recv_sem=ring_recv.at[line, way, part, step],
            device_id=(w, right if way == 0 else left),
            device_id_type=MESH,
        )

    def steps_of(line, way, part):
        return half if (way == part) == (line == 0) else half - 1

    def begin(line, part):
        for way in (0, 1):
            ring(line, way, part, 1).start()

    def advance(line, step, part):
        for way in (0, 1):
            if isinstance(step, int) and step > steps_of(line, way, part):
                continue
            ring(line, way, part, step).wait_recv()
            if not isinstance(step, int) or step < steps_of(line, way, part):
                ring(line, way, part, step + 1).start()

    def wide_start(src, dst, k, peer):
        @pl.when(peer != w)
        def _():
            pltpu.make_async_remote_copy(
                src_ref=src.at[peer],
                dst_ref=dst.at[w],
                send_sem=wide_send.at[k],
                recv_sem=wide_recv.at[k],
                device_id=(peer, g),
                device_id_type=MESH,
            ).start()

        @pl.when(peer == w)
        def _():
            pltpu.make_async_copy(src.at[w], dst.at[w], wide_recv.at[k]).start()

    def wide_arrived(dst, k):
        pltpu.make_async_copy(dst, dst, wide_recv.at[k]).wait()

    def wide_drain(src, k):
        others = src.at[pl.ds(0, n_w - 1)]
        pltpu.make_async_copy(others, others, wide_send.at[k]).wait()

    loads[0].wait()
    pl.semaphore_wait(barrier, n_g - 1 + n_w - 1)
    begin(0, 0)
    begin(0, 1)

    owner = lax.broadcasted_iota(jnp.int32, (slots, n_w), 1)
    slot = lax.broadcasted_iota(jnp.int32, (slots, n_w), 0)
    spread = as_bf16(lax.div(slot, cap) == owner)
    picks = send_rows[...]
    high = (picks & ~15).astype(F32).astype(BF16)
    low = (picks & 15).astype(F32).astype(BF16)
    place = lax.broadcasted_iota(jnp.int32, (slots, cap), 1)
    slot = lax.broadcasted_iota(jnp.int32, (slots, cap), 0)
    mine = lax.rem(slot, cap) == place
    high = jnp.where(mine, dot(spread, high, NT), 0.0).astype(BF16)
    low = jnp.where(mine, dot(spread, low, NT), 0.0).astype(BF16)
    ones = jnp.ones((cap, table_rows), BF16)
    row_of = dot(high, ones) + dot(low, ones)
    row = lax.broadcasted_iota(jnp.int32, (slots, table_rows), 1).astype(F32)
    pick = as_bf16(row_of == row)
    loads[2].wait()
    fetched = dot(pick, table[...].astype(BF16)).astype(BF16)
    cold_out[...] = fetched.reshape(n_w, cap, depth)

    loads[1].wait()
    begin(1, 0)

    per = n_w // cold_blocks

    def send_cold(k):
        @pl.loop(0, per)
        def _(j):
            wide_start(cold_out, cold_keys, 0, lax.rem(w + 1 + k * per + j, n_w))

    send_cold(0)
    query_t[...] = jnp.transpose(line_q[0])

    def fold(s, first=False):
        s3 = s.reshape(s.shape[0] // 8, 8, s.shape[1])
        top = jnp.max(s3, axis=0)
        if first:
            top8[...] = top
            sum8[...] = jnp.sum(jnp.exp(s3 - top[None]), axis=0)
        else:
            before = top8[...]
            top = jnp.maximum(before, top)
            top8[...] = top
            sum8[...] = sum8[...] * jnp.exp(before - top) + jnp.sum(jnp.exp(s3 - top[None]), axis=0)

    def score(block, part=None):
        at = slice(None) if part is None else pl.ds(part * chunk, chunk)
        s = dot(keys[block, at], query_t[...]) * scale
        s_in[block, at] = s
        fold(s, first=part is None)

    def score_cold(k):
        at = pl.ds(k * cold_rows, cold_rows)
        owner = lax.broadcasted_iota(jnp.int32, (cold_rows, n_w), 1)
        slot = lax.broadcasted_iota(jnp.int32, (cold_rows, n_w), 0) + k * cold_rows
        spread = as_bf16(lax.div(slot, cap) == owner)
        counts = jnp.broadcast_to(live_counts[...].astype(F32).astype(BF16), (rows, n_w))
        counts = dot(spread, counts, NT)
        place = lax.rem(lax.broadcasted_iota(jnp.int32, (cold_rows, rows), 0), cap).astype(F32)
        owners = pl.ds(k * (n_w // cold_blocks), n_w // cold_blocks)
        found = cold_keys[owners].reshape(cold_rows, depth)
        s = dot(found, query_t[...]) * scale
        s = jnp.where(place < counts, s, -jnp.inf)
        s_cold[at] = s
        fold(s)


    score(0)

    def score_query(step, part):
        for way in (0, 1):
            if isinstance(step, int) and step > steps_of(1, way, part):
                continue
            block = step if way == 0 else n_g - step
            found = line_q[block, pl.ds(part * chunk, chunk)]
            s_back[block, :, pl.ds(part * chunk, chunk)] = dot(keys[0], found, NT) * scale

    looped = max(half - 2, 0)
    cold_first = half - 1 - (cold_blocks + 1) // 2
    in_loop = looped >= cold_blocks and cold_first > (cold_blocks + 1) // 2

    if not in_loop:
        for k in range(1, cold_blocks):
            send_cold(k)

    def items_step(n):
        for part in (0, 1):
            advance(0, n, part)
            if in_loop and not isinstance(n, int):
                k = 2 * (n - 1) + part + 1

                @pl.when(k < cold_blocks)
                def _():
                    send_cold(k)

                if part == 0:

                    @pl.when(n == cold_first)
                    def _():
                        wide_arrived(cold_keys, 0)

                k = 2 * (n - cold_first) + part

                @pl.when((k >= 0) & (k < cold_blocks))
                def _():
                    score_cold(k)

            score(n, part)
            if not isinstance(n, int) or n < half:
                score(n_g - n, part)

    begun = looped // 2

    @pl.loop(0, begun)
    def _(m):
        items_step(2 * m + 1)

        @pl.when(m == 0)
        def _():
            begin(1, 1)

        advance(1, m + 1, 0)
        score_query(m + 1, 0)
        items_step(2 * m + 2)
        advance(1, m + 1, 1)
        score_query(m + 1, 1)

    if begun == 0:
        begin(1, 1)

    if not in_loop:
        wide_arrived(cold_keys, 0)
        for k in range(cold_blocks):
            score_cold(k)

    queue = [(m, part) for m in range(begun + 1, half + 1) for part in (0, 1)]
    passed = []

    def query_step():
        if queue:
            step, part = queue.pop(0)
            advance(1, step, part)
            score_query(step, part)
            passed.append((step, part))

    for n in range(2 * begun + 1, half + 1):
        items_step(n)
        if n < half or half > 2:
            query_step()

    top = jnp.max(top8[...], axis=0, keepdims=True)
    total = jnp.sum(sum8[...] * jnp.exp(top8[...] - top), axis=0, keepdims=True)
    lse_all[0] = top + jnp.log(total)

    def lse_copy(p):
        return pltpu.make_async_remote_copy(
            src_ref=lse_all.at[0],
            dst_ref=lse_all.at[p],
            send_sem=lse_send.at[p],
            recv_sem=lse_recv.at[p],
            device_id=(w, lax.rem(g + p, n_g)),
            device_id_type=MESH,
        )

    @pl.loop(1, n_g)
    def _(p):
        lse_copy(p).start()

    own_part = lax.div(w, per)

    def send_back(i):
        k = lax.rem(own_part + i, cold_blocks)
        at = pl.ds(pl.multiple_of(k * cold_rows, cold_rows), cold_rows)
        d = jnp.exp(s_cold[at] - lse_all[0]).astype(BF16)
        back = (dot(d, line_q[0]) * scale).astype(BF16)
        slot_out[pl.ds(k * per, per)] = back.reshape(per, cap, depth)

        @pl.loop(0, per)
        def _(j):
            wide_start(slot_out, slot_back, 1, k * per + lax.rem(w + j, per))

    for i in range(cold_blocks):
        send_back(i)
        if i % 2 == 1:
            query_step()

    d = jnp.exp(s_in[0] - lse_all[0])
    key = lax.broadcasted_iota(jnp.int32, d.shape, 0)
    query = lax.broadcasted_iota(jnp.int32, d.shape, 1)
    d = (d - jnp.where(key == query, 1.0, 0.0)).astype(BF16)
    query_grad[...] = dot(d, keys[0], TN)
    item_grad[...] = dot(d, line_q[0])

    jobs = n_g - 1 + cold_blocks

    def to_queries(i):
        @pl.when(i < n_g - 1)
        def _():
            d = jnp.exp(s_in[1 + i] - lse_all[0]).astype(BF16)
            query_grad[...] += dot(d, keys[1 + i], TN)

        @pl.when((i >= n_g - 1) & (i < jobs))
        def _():
            k = i - (n_g - 1)
            d = jnp.exp(s_cold[pl.ds(k * cold_rows, cold_rows)] - lse_all[0]).astype(BF16)
            found = cold_keys[pl.ds(k * per, per)].reshape(cold_rows, depth)
            query_grad[...] += dot(d, found, TN)

    def to_items(block):
        d = jnp.exp(s_back[block] - lse_all[block]).astype(BF16)
        item_grad[...] += dot(d, line_q[block])

    owner = lax.broadcasted_iota(jnp.int32, (n_w, slots), 0)
    slot = lax.broadcasted_iota(jnp.int32, (n_w, slots), 1)
    spread = as_bf16(lax.div(slot, cap) == owner)
    picks = send_rows[...]
    high = dot((picks & ~15).astype(F32).astype(BF16), spread)
    low = dot((picks & 15).astype(F32).astype(BF16), spread)
    place = lax.broadcasted_iota(jnp.int32, (cap, slots), 0)
    slot = lax.broadcasted_iota(jnp.int32, (cap, slots), 1)
    row_of = jnp.sum(
        jnp.where(lax.rem(slot, cap) == place, high + low, 0.0), axis=0, keepdims=True
    )
    row = lax.broadcasted_iota(jnp.int32, (table_rows, slots), 0).astype(F32)
    put[...] = as_bf16(row_of == row)

    @pl.loop(1, n_g)
    def _(p):
        lse_copy(p).wait_recv()

    whole = passed[-1][0] - (1 if passed[-1][1] == 0 else 0) if passed else begun
    ready = [(step, n_g - step) for step in range(1, whole + 1)]
    left_over = [jobs * i // max(len(queue) - 1, 1) for i in range(max(len(queue), 1) + 1)]
    turn = 0
    while len(queue) > 1:

        @pl.loop(left_over[turn], left_over[turn + 1])
        def _(i):
            to_queries(i)

        if ready:
            for block in ready.pop(0):
                to_items(block)
        query_step()
        step, part = passed[-1]
        if part == 1:
            ready.append((step, n_g - step))
        turn += 1

    @pl.loop(left_over[turn], jobs)
    def _(i):
        to_queries(i)

    for blocks in ready:
        for block in blocks:
            to_items(block)

    query_grad[...] = query_grad[...] * scale
    saves[0].start()
    def update():
        wide_arrived(slot_back, 1)
        loads[3].wait()
        grad = dot(put[...], slot_back[...].reshape(slots, depth))
        new_table[...] = table[...] - 0.5 * grad / jnp.sqrt(accum[...] + grad * grad)
        saves[2].start()

    update()
    while queue:
        query_step()
    to_items(half)
    item_grad[...] = item_grad[...] * scale
    saves[1].start()

    wide_drain(cold_out, 0)
    wide_drain(slot_out, 1)

    @pl.loop(1, n_g)
    def _(p):
        lse_copy(p).wait_send()

    for way in (0, 1):
        for part in (0, 1):

            for line in (0, 1):

                @pl.loop(1, steps_of(line, way, part) + 1)
                def _(n):
                    ring(line, way, part, n).wait_send()

    for save in saves:
        save.wait()


def store(*refs):
    here, there, held, sems = refs[:3], refs[3:6], refs[6:9], refs[9]
    for i in range(3):
        pltpu.make_async_copy(here[i], held[i], sems.at[0, i]).start()
    for i in range(3):
        pltpu.make_async_copy(here[i], held[i], sems.at[0, i]).wait()
        pltpu.make_async_copy(held[i], there[i], sems.at[1, i]).start()
    for i in range(3):
        pltpu.make_async_copy(held[i], there[i], sems.at[1, i]).wait()


def on_device(n_w, n_g, queries, items, cold_table, accum, send_rows, live_counts):
    rows, depth = queries.shape
    table_rows = cold_table.shape[0]
    cap = send_rows.shape[1]
    slots = n_w * cap
    half = n_g // 2
    vmem = pl.BlockSpec(memory_space=pltpu.VMEM)
    hbm = pl.BlockSpec(memory_space=pl.ANY)
    limit = 60 * 1024 * 1024
    ring_sems = pltpu.SemaphoreType.DMA((2, 2, 2, half + 1))
    results = pl.pallas_call(
        functools.partial(kernel, n_w, n_g, cap),
        out_shape=(
            jax.ShapeDtypeStruct((rows, depth), F32),
            jax.ShapeDtypeStruct((rows, depth), F32),
            jax.ShapeDtypeStruct((table_rows, depth), F32),
        ),
        in_specs=[hbm, hbm, hbm, hbm, vmem, vmem],
        out_specs=(hbm, hbm, hbm),
        scratch_shapes=[
            pltpu.VMEM((rows, depth), F32),
            pltpu.VMEM((rows, depth), F32),
            pltpu.VMEM((table_rows, depth), F32),
            pltpu.VMEM((n_g, rows, depth), BF16),
            pltpu.VMEM((n_g, rows, depth), BF16),
            pltpu.VMEM((n_g, 1, rows), F32),
            pltpu.VMEM((n_g, rows, rows), F32),
            pltpu.VMEM((n_g, rows, rows), F32),
            pltpu.VMEM((slots, rows), F32),
            pltpu.VMEM((8, rows), F32),
            pltpu.VMEM((8, rows), F32),
            pltpu.VMEM((table_rows, depth), F32),
            pltpu.VMEM((table_rows, depth), F32),
            pltpu.VMEM((n_w, cap, depth), BF16),
            pltpu.VMEM((n_w, cap, depth), BF16),
            pltpu.VMEM((n_w, cap, depth), BF16),
            pltpu.VMEM((n_w, cap, depth), BF16),
            pltpu.VMEM((depth, rows), BF16),
            pltpu.VMEM((table_rows, slots), BF16),
            pltpu.SemaphoreType.DMA((4,)),
            pltpu.SemaphoreType.DMA((3,)),
            ring_sems,
            ring_sems,
            pltpu.SemaphoreType.DMA((n_g,)),
            pltpu.SemaphoreType.DMA((n_g,)),
            pltpu.SemaphoreType.DMA((2,)),
            pltpu.SemaphoreType.DMA((2,)),
        ],
        compiler_params=pltpu.CompilerParams(
            collective_id=0, has_side_effects=True, vmem_limit_bytes=limit
        ),
    )(queries, items, cold_table, accum, send_rows.T, live_counts)
    return pl.pallas_call(
        store,
        out_shape=tuple(jax.ShapeDtypeStruct(r.shape, r.dtype) for r in results),
        in_specs=[hbm] * 3,
        out_specs=(hbm,) * 3,
        scratch_shapes=[pltpu.VMEM(r.shape, r.dtype) for r in results]
        + [pltpu.SemaphoreType.DMA((2, 3))],
        compiler_params=pltpu.CompilerParams(vmem_limit_bytes=limit),
    )(*results)


def solution(mesh):
    spec = P(("wide", "group"), None)
    return jax.shard_map(
        functools.partial(on_device, mesh.shape["wide"], mesh.shape["group"]),
        mesh=mesh,
        in_specs=(spec,) * 6,
        out_specs=(spec,) * 3,
        check_vma=False,
    )
```

```python
import functools

import jax
import jax.numpy as jnp
from jax import lax
from jax.experimental import pallas as pl
from jax.experimental.pallas import tpu as pltpu
from jax.sharding import PartitionSpec as P

MESH = pl.DeviceIdType.MESH
NT = (((1,), (1,)), ((), ()))
TN = (((0,), (0,)), ((), ()))
F32 = jnp.float32
BF16 = jnp.bfloat16
PARTS = 2
RATE = (1, 2)


def dot(a, b, dims=(((1,), (0,)), ((), ()))):
    return lax.dot_general(a, b, dims, preferred_element_type=F32)


def as_bf16(condition):
    return jnp.where(condition, 1.0, 0.0).astype(BF16)


def kernel(
    n_w,
    n_g,
    cap,
    queries,
    items,
    table_hbm,
    accum_hbm,
    send_rows,
    live_counts,
    query_grad,
    item_grad,
    new_table,
    keys,
    line_q,
    lse_all,
    s_in,
    s_back,
    s_cold,
    top8,
    sum8,
    table,
    accum,
    cold_out,
    cold_keys,
    slot_out,
    slot_back,
    query_t,
    put,
    load_sem,
    ring_send,
    ring_recv,
    lse_send,
    lse_recv,
    wide_send,
    wide_recv,
):
    w, g = lax.axis_index("wide"), lax.axis_index("group")
    right, left = lax.rem(g + 1, n_g), lax.rem(g + n_g - 1, n_g)
    half = n_g // 2
    rows, depth = queries.shape
    chunk = rows // PARTS
    slots = n_w * cap
    table_rows = table.shape[0]
    scale = depth ** (-0.5)
    cold_blocks = max(slots // 256, 1)
    cold_rows = slots // cold_blocks
    per = n_w // cold_blocks

    loads = [
        pltpu.make_async_copy(items, keys.at[0], load_sem.at[0]),
        pltpu.make_async_copy(queries, line_q.at[0], load_sem.at[1]),
        pltpu.make_async_copy(table_hbm, table, load_sem.at[2]),
        pltpu.make_async_copy(accum_hbm, accum, load_sem.at[3]),
    ]
    for load in loads:
        load.start()

    barrier = pltpu.get_barrier_semaphore()

    @pl.loop(1, n_g)
    def _(p):
        pl.semaphore_signal(
            barrier, inc=1, device_id=(w, lax.rem(g + p, n_g)), device_id_type=MESH
        )

    @pl.loop(1, n_w)
    def _(p):
        pl.semaphore_signal(
            barrier, inc=1, device_id=(lax.rem(w + p, n_w), g), device_id_type=MESH
        )

    def ring(line, way, part, step):
        at = pl.ds(pl.multiple_of(part * chunk, chunk), chunk)
        src, dst = (step - 1, step) if way == 0 else (lax.rem(n_g + 1 - step, n_g), n_g - step)
        buffer = line_q if line else keys
        return pltpu.make_async_remote_copy(
            src_ref=buffer.at[src, at],
            dst_ref=buffer.at[dst, at],
            send_sem=ring_send.at[line, way, part, step],
            recv_sem=ring_recv.at[line, way, part, step],
            device_id=(w, right if way == 0 else left),
            device_id_type=MESH,
        )

    def steps_of(line, way, part):
        return half if (way == 0) == ((part < PARTS // 2) == (line == 0)) else half - 1

    def begin(line, part):
        for way in (0, 1):
            ring(line, way, part, 1).start()

    def advance(line, step, part):
        for way in (0, 1):
            if isinstance(step, int) and step > steps_of(line, way, part):
                continue
            ring(line, way, part, step).wait_recv()
            if not isinstance(step, int) or step < steps_of(line, way, part):
                ring(line, way, part, step + 1).start()

    def wide_start(src, dst, k, peer):
        @pl.when(peer != w)
        def _():
            pltpu.make_async_remote_copy(
                src_ref=src.at[peer],
                dst_ref=dst.at[w],
                send_sem=wide_send.at[k],
                recv_sem=wide_recv.at[k],
                device_id=(peer, g),
                device_id_type=MESH,
            ).start()

        @pl.when(peer == w)
        def _():
            pltpu.make_async_copy(src.at[w], dst.at[w], wide_recv.at[k]).start()

    def wide_part(src, dst, k, part):
        @pl.loop(part * per, part * per + per)
        def _(j):
            away = (j + 1) // 2
            wide_start(src, dst, k, lax.rem(w + jnp.where(lax.rem(j, 2) == 0, away, n_w - away), n_w))

    def wide_arrived(dst, k):
        pltpu.make_async_copy(dst, dst, wide_recv.at[k]).wait()

    def wide_drain(src, k):
        others = src.at[pl.ds(0, n_w - 1)]
        pltpu.make_async_copy(others, others, wide_send.at[k]).wait()

    loads[0].wait()
    pl.semaphore_wait(barrier, n_g - 1 + n_w - 1)
    for part in range(PARTS):
        begin(0, part)

    owner = lax.broadcasted_iota(jnp.int32, (slots, n_w), 1)
    slot = lax.broadcasted_iota(jnp.int32, (slots, n_w), 0)
    spread = as_bf16(lax.div(slot, cap) == owner)
    picks = send_rows[...]
    high = (picks & ~15).astype(F32).astype(BF16)
    low = (picks & 15).astype(F32).astype(BF16)
    place = lax.broadcasted_iota(jnp.int32, (slots, cap), 1)
    slot = lax.broadcasted_iota(jnp.int32, (slots, cap), 0)
    mine = lax.rem(slot, cap) == place
    high = jnp.where(mine, dot(spread, high, NT), 0.0).astype(BF16)
    low = jnp.where(mine, dot(spread, low, NT), 0.0).astype(BF16)
    ones = jnp.ones((cap, table_rows), BF16)
    row_of = dot(high, ones) + dot(low, ones)
    row = lax.broadcasted_iota(jnp.int32, (slots, table_rows), 1).astype(F32)
    pick = as_bf16(row_of == row)
    loads[2].wait()
    fetched = dot(pick, table[...].astype(BF16)).astype(BF16)
    cold_out[...] = fetched.reshape(n_w, cap, depth)

    loads[1].wait()
    for part in range(PARTS):
        begin(1, part)

    def send_cold(k):
        wide_part(cold_out, cold_keys, 0, k)

    send_cold(0)
    query_t[...] = jnp.transpose(line_q[0])

    def fold(s, first=False):
        s3 = s.reshape(s.shape[0] // 8, 8, s.shape[1])
        top = jnp.max(s3, axis=0)
        if first:
            top8[...] = top
            sum8[...] = jnp.sum(jnp.exp(s3 - top[None]), axis=0)
        else:
            before = top8[...]
            top = jnp.maximum(before, top)
            top8[...] = top
            sum8[...] = sum8[...] * jnp.exp(before - top) + jnp.sum(jnp.exp(s3 - top[None]), axis=0)

    def score(block, first=False):
        s = dot(keys[block], query_t[...]) * scale
        s_in[block] = s
        fold(s, first)

    def score_cold(k):
        at = pl.ds(k * cold_rows, cold_rows)
        owner = lax.broadcasted_iota(jnp.int32, (cold_rows, n_w), 1)
        slot = lax.broadcasted_iota(jnp.int32, (cold_rows, n_w), 0) + k * cold_rows
        spread = as_bf16(lax.div(slot, cap) == owner)
        counts = jnp.broadcast_to(live_counts[...].astype(F32).astype(BF16), (rows, n_w))
        counts = dot(spread, counts, NT)
        place = lax.rem(lax.broadcasted_iota(jnp.int32, (cold_rows, rows), 0), cap).astype(F32)
        owners = pl.ds(k * (n_w // cold_blocks), n_w // cold_blocks)
        found = cold_keys[owners].reshape(cold_rows, depth)
        s = dot(found, query_t[...]) * scale
        s = jnp.where(place < counts, s, -jnp.inf)
        s_cold[at] = s
        fold(s)


    score(0, first=True)

    def score_query(step):
        for block in {step, n_g - step} if isinstance(step, int) else (step, n_g - step):
            s_back[block] = dot(keys[0], line_q[block], NT) * scale

    looped = max(half - 2, 0)
    cold_first = half - 1 - (cold_blocks + 1) // 2
    in_loop = looped >= cold_blocks and cold_first > (cold_blocks + 1) // 2

    if not in_loop:
        for k in range(1, cold_blocks):
            send_cold(k)

    def items_work(n):
        for part in (0, 1):
            if in_loop and not isinstance(n, int):
                k = 2 * (n - 1) + part + 1

                @pl.when(k < cold_blocks)
                def _():
                    send_cold(k)

                if part == 0:

                    @pl.when(n == cold_first)
                    def _():
                        wide_arrived(cold_keys, 0)

                k = 2 * (n - cold_first) + part

                @pl.when((k >= 0) & (k < cold_blocks))
                def _():
                    score_cold(k)

        score(n)
        if not isinstance(n, int) or n < half:
            score(n_g - n)

    def passed_by(n):
        return PARTS * n * RATE[0] // RATE[1]

    @pl.loop(1, half - 1)
    def _(n):
        for part in range(PARTS):
            advance(0, n, part)

        @pl.loop(passed_by(n - 1), passed_by(n))
        def _(e):
            advance(1, e // PARTS + 1, lax.rem(e, PARTS))

        items_work(n)

        @pl.when(passed_by(n) // PARTS > passed_by(n - 1) // PARTS)
        def _():
            score_query(passed_by(n) // PARTS)

    if not in_loop:
        wide_arrived(cold_keys, 0)
        for k in range(cold_blocks):
            score_cold(k)

    events = [(m, part) for m in range(1, half + 1) for part in range(PARTS)]
    queue = events[passed_by(looped) :]
    passed = events[: passed_by(looped)]

    def query_step():
        if queue:
            step, part = queue.pop(0)
            advance(1, step, part)
            passed.append((step, part))
            if part == PARTS - 1:
                score_query(step)

    for n in range(looped + 1, half + 1):
        for part in range(PARTS):
            advance(0, n, part)
        items_work(n)
        for _ in range(passed_by(n) - passed_by(n - 1)):
            query_step()

    top = jnp.max(top8[...], axis=0, keepdims=True)
    total = jnp.sum(sum8[...] * jnp.exp(top8[...] - top), axis=0, keepdims=True)
    lse_all[0] = top + jnp.log(total)

    def lse_copy(p):
        return pltpu.make_async_remote_copy(
            src_ref=lse_all.at[0],
            dst_ref=lse_all.at[p],
            send_sem=lse_send.at[p],
            recv_sem=lse_recv.at[p],
            device_id=(w, lax.rem(g + p, n_g)),
            device_id_type=MESH,
        )

    @pl.loop(1, n_g)
    def _(p):
        lse_copy(p).start()

    @pl.loop(0, cold_blocks)
    def _(k):
        d = jnp.exp(s_cold[pl.ds(k * cold_rows, cold_rows)] - lse_all[0]).astype(BF16)
        back = (dot(d, line_q[0]) * scale).astype(BF16)
        slot_out[pl.ds(k * per, per)] = back.reshape(per, cap, depth)

    for i in range(cold_blocks):
        wide_part(slot_out, slot_back, 1, i)
        for _ in range(max(PARTS // 4, 1)):
            query_step()

    d = jnp.exp(s_in[0] - lse_all[0])
    key = lax.broadcasted_iota(jnp.int32, d.shape, 0)
    query = lax.broadcasted_iota(jnp.int32, d.shape, 1)
    d = (d - jnp.where(key == query, 1.0, 0.0)).astype(BF16)
    query_grad[...] = dot(d, keys[0], TN)
    item_grad[...] = dot(d, line_q[0])

    jobs = n_g - 1 + cold_blocks

    def to_queries(i):
        @pl.when(i < n_g - 1)
        def _():
            d = jnp.exp(s_in[1 + i] - lse_all[0]).astype(BF16)
            query_grad[...] += dot(d, keys[1 + i], TN)

        @pl.when((i >= n_g - 1) & (i < jobs))
        def _():
            k = i - (n_g - 1)
            d = jnp.exp(s_cold[pl.ds(k * cold_rows, cold_rows)] - lse_all[0]).astype(BF16)
            found = cold_keys[pl.ds(k * per, per)].reshape(cold_rows, depth)
            query_grad[...] += dot(d, found, TN)

    def to_items(block):
        d = jnp.exp(s_back[block] - lse_all[block]).astype(BF16)
        item_grad[...] += dot(d, line_q[block])

    owner = lax.broadcasted_iota(jnp.int32, (n_w, slots), 0)
    slot = lax.broadcasted_iota(jnp.int32, (n_w, slots), 1)
    spread = as_bf16(lax.div(slot, cap) == owner)
    picks = send_rows[...]
    high = dot((picks & ~15).astype(F32).astype(BF16), spread)
    low = dot((picks & 15).astype(F32).astype(BF16), spread)
    place = lax.broadcasted_iota(jnp.int32, (cap, slots), 0)
    slot = lax.broadcasted_iota(jnp.int32, (cap, slots), 1)
    row_of = jnp.sum(
        jnp.where(lax.rem(slot, cap) == place, high + low, 0.0), axis=0, keepdims=True
    )
    row = lax.broadcasted_iota(jnp.int32, (table_rows, slots), 0).astype(F32)
    put[...] = as_bf16(row_of == row)

    @pl.loop(1, n_g)
    def _(p):
        lse_copy(p).wait_recv()

    whole = min(len(passed) // PARTS, half - 1)
    ready = [(step, n_g - step) for step in range(1, whole + 1)]
    turns = max(len(queue) - PARTS // 2, 0)
    for turn in range(turns):

        @pl.loop(jobs * turn // turns, jobs * (turn + 1) // turns)
        def _(i):
            to_queries(i)

        query_step()
        if ready and 2 * turn >= turns * (whole - len(ready)) // max(whole, 1):
            for block in ready.pop(0):
                to_items(block)
        step, part = passed[-1]
        if part == PARTS - 1 and step < half:
            ready.append((step, n_g - step))

    if turns == 0:

        @pl.loop(0, jobs)
        def _(i):
            to_queries(i)

    for blocks in ready:
        for block in blocks:
            to_items(block)

    query_grad[...] = query_grad[...] * scale

    def update():
        wide_arrived(slot_back, 1)
        loads[3].wait()
        grad = dot(put[...], slot_back[...].reshape(slots, depth))
        new_table[...] = table[...] - 0.5 * grad / jnp.sqrt(accum[...] + grad * grad)

    update()
    while queue:
        query_step()
        step, part = passed[-1]
        if part == PARTS - 1 and step < half:
            to_items(step)
            to_items(n_g - step)
    to_items(half)
    item_grad[...] = item_grad[...] * scale

    wide_drain(cold_out, 0)
    wide_drain(slot_out, 1)

    @pl.loop(1, n_g)
    def _(p):
        lse_copy(p).wait_send()

    for way in (0, 1):
        for part in range(PARTS):
            for line in (0, 1):

                @pl.loop(1, steps_of(line, way, part) + 1)
                def _(n):
                    ring(line, way, part, n).wait_send()


def store(*refs):
    sems = refs[-1]
    copies = [pltpu.make_async_copy(refs[i], refs[3 + i], sems.at[i]) for i in range(3)]
    for copy in copies:
        copy.start()
    for copy in copies:
        copy.wait()


def on_device(n_w, n_g, queries, items, cold_table, accum, send_rows, live_counts):
    rows, depth = queries.shape
    table_rows = cold_table.shape[0]
    cap = send_rows.shape[1]
    slots = n_w * cap
    half = n_g // 2
    vmem = pl.BlockSpec(memory_space=pltpu.VMEM)
    hbm = pl.BlockSpec(memory_space=pl.ANY)
    limit = 60 * 1024 * 1024
    ring_sems = pltpu.SemaphoreType.DMA((2, 2, PARTS, half + 1))
    results = pl.pallas_call(
        functools.partial(kernel, n_w, n_g, cap),
        out_shape=(
            pltpu.VMEM((rows, depth), F32),
            pltpu.VMEM((rows, depth), F32),
            pltpu.VMEM((table_rows, depth), F32),
        ),
        in_specs=[hbm, hbm, hbm, hbm, vmem, vmem],
        out_specs=(vmem, vmem, vmem),
        scratch_shapes=[
            pltpu.VMEM((n_g, rows, depth), BF16),
            pltpu.VMEM((n_g, rows, depth), BF16),
            pltpu.VMEM((n_g, 1, rows), F32),
            pltpu.VMEM((n_g, rows, rows), F32),
            pltpu.VMEM((n_g, rows, rows), F32),
            pltpu.VMEM((slots, rows), F32),
            pltpu.VMEM((8, rows), F32),
            pltpu.VMEM((8, rows), F32),
            pltpu.VMEM((table_rows, depth), F32),
            pltpu.VMEM((table_rows, depth), F32),
            pltpu.VMEM((n_w, cap, depth), BF16),
            pltpu.VMEM((n_w, cap, depth), BF16),
            pltpu.VMEM((n_w, cap, depth), BF16),
            pltpu.VMEM((n_w, cap, depth), BF16),
            pltpu.VMEM((depth, rows), BF16),
            pltpu.VMEM((table_rows, slots), BF16),
            pltpu.SemaphoreType.DMA((4,)),
            ring_sems,
            ring_sems,
            pltpu.SemaphoreType.DMA((n_g,)),
            pltpu.SemaphoreType.DMA((n_g,)),
            pltpu.SemaphoreType.DMA((2,)),
            pltpu.SemaphoreType.DMA((2,)),
        ],
        compiler_params=pltpu.CompilerParams(
            collective_id=0, has_side_effects=True, vmem_limit_bytes=limit
        ),
    )(queries, items, cold_table, accum, send_rows.T, live_counts)
    return pl.pallas_call(
        store,
        out_shape=tuple(jax.ShapeDtypeStruct(r.shape, r.dtype) for r in results),
        in_specs=[hbm] * 3,
        out_specs=(hbm,) * 3,
        scratch_shapes=[pltpu.SemaphoreType.DMA((3,))],
        compiler_params=pltpu.CompilerParams(vmem_limit_bytes=4 * 1024 * 1024),
    )(*results)


def solution(mesh):
    spec = P(("wide", "group"), None)
    return jax.shard_map(
        functools.partial(on_device, mesh.shape["wide"], mesh.shape["group"]),
        mesh=mesh,
        in_specs=(spec,) * 6,
        out_specs=(spec,) * 3,
        check_vma=False,
    )
```

```python
import functools

import jax
import jax.numpy as jnp
from jax import lax
from jax.experimental import pallas as pl
from jax.experimental.pallas import tpu as pltpu
from jax.sharding import PartitionSpec as P

MESH = pl.DeviceIdType.MESH
NT = (((1,), (1,)), ((), ()))
TN = (((0,), (0,)), ((), ()))
F32 = jnp.float32
BF16 = jnp.bfloat16
PARTS = 2
RATE = (7, 16)


def dot(a, b, dims=(((1,), (0,)), ((), ()))):
    return lax.dot_general(a, b, dims, preferred_element_type=F32)


def as_bf16(condition):
    return jnp.where(condition, 1.0, 0.0).astype(BF16)


def kernel(
    n_w,
    n_g,
    cap,
    queries,
    items,
    table_hbm,
    accum_hbm,
    send_rows,
    live_counts,
    query_grad,
    item_grad,
    new_table,
    keys,
    line_q,
    lse_all,
    s_in,
    s_back,
    s_cold,
    top8,
    sum8,
    table,
    accum,
    cold_out,
    cold_keys,
    slot_out,
    slot_back,
    query_t,
    put,
    load_sem,
    ring_send,
    ring_recv,
    lse_send,
    lse_recv,
    wide_send,
    wide_recv,
):
    w, g = lax.axis_index("wide"), lax.axis_index("group")
    right, left = lax.rem(g + 1, n_g), lax.rem(g + n_g - 1, n_g)
    half = n_g // 2
    rows, depth = queries.shape
    chunk = rows // PARTS
    slots = n_w * cap
    table_rows = table.shape[0]
    scale = depth ** (-0.5)
    cold_blocks = max(slots // 256, 1)
    cold_rows = slots // cold_blocks
    per = n_w // cold_blocks

    loads = [
        pltpu.make_async_copy(items, keys.at[0], load_sem.at[0]),
        pltpu.make_async_copy(queries, line_q.at[0], load_sem.at[1]),
        pltpu.make_async_copy(table_hbm, table, load_sem.at[2]),
        pltpu.make_async_copy(accum_hbm, accum, load_sem.at[3]),
    ]
    for load in loads:
        load.start()

    barrier = pltpu.get_barrier_semaphore()

    @pl.loop(1, n_g)
    def _(p):
        pl.semaphore_signal(
            barrier, inc=1, device_id=(w, lax.rem(g + p, n_g)), device_id_type=MESH
        )

    @pl.loop(1, n_w)
    def _(p):
        pl.semaphore_signal(
            barrier, inc=1, device_id=(lax.rem(w + p, n_w), g), device_id_type=MESH
        )

    def ring(line, way, part, step):
        at = pl.ds(pl.multiple_of(part * chunk, chunk), chunk)
        src, dst = (step - 1, step) if way == 0 else (lax.rem(n_g + 1 - step, n_g), n_g - step)
        buffer = line_q if line else keys
        return pltpu.make_async_remote_copy(
            src_ref=buffer.at[src, at],
            dst_ref=buffer.at[dst, at],
            send_sem=ring_send.at[line, way, part, step],
            recv_sem=ring_recv.at[line, way, part, step],
            device_id=(w, right if way == 0 else left),
            device_id_type=MESH,
        )

    def steps_of(line, way, part):
        return half if (way == 0) == ((part < PARTS // 2) == (line == 0)) else half - 1

    def begin(line, part):
        for way in (0, 1):
            ring(line, way, part, 1).start()

    def advance(line, step, part):
        for way in (0, 1):
            if isinstance(step, int) and step > steps_of(line, way, part):
                continue
            ring(line, way, part, step).wait_recv()
            if not isinstance(step, int) or step < steps_of(line, way, part):
                ring(line, way, part, step + 1).start()

    def wide_start(src, dst, k, peer):
        @pl.when(peer != w)
        def _():
            pltpu.make_async_remote_copy(
                src_ref=src.at[peer],
                dst_ref=dst.at[w],
                send_sem=wide_send.at[k],
                recv_sem=wide_recv.at[k],
                device_id=(peer, g),
                device_id_type=MESH,
            ).start()

        @pl.when(peer == w)
        def _():
            pltpu.make_async_copy(src.at[w], dst.at[w], wide_recv.at[k]).start()

    def wide_part(src, dst, k, part):
        @pl.loop(part * per, part * per + per)
        def _(j):
            away = (j + 1) // 2
            wide_start(src, dst, k, lax.rem(w + jnp.where(lax.rem(j, 2) == 0, away, n_w - away), n_w))

    def wide_arrived(dst, k):
        pltpu.make_async_copy(dst, dst, wide_recv.at[k]).wait()

    def wide_drain(src, k):
        others = src.at[pl.ds(0, n_w - 1)]
        pltpu.make_async_copy(others, others, wide_send.at[k]).wait()

    loads[0].wait()
    pl.semaphore_wait(barrier, n_g - 1 + n_w - 1)
    for part in range(PARTS):
        begin(0, part)
    loads[1].wait()
    for part in range(PARTS):
        begin(1, part)

    owner = lax.broadcasted_iota(jnp.int32, (slots, n_w), 1)
    slot = lax.broadcasted_iota(jnp.int32, (slots, n_w), 0)
    spread = as_bf16(lax.div(slot, cap) == owner)
    picks = send_rows[...]
    high = (picks & ~15).astype(F32).astype(BF16)
    low = (picks & 15).astype(F32).astype(BF16)
    place = lax.broadcasted_iota(jnp.int32, (slots, cap), 1)
    slot = lax.broadcasted_iota(jnp.int32, (slots, cap), 0)
    mine = lax.rem(slot, cap) == place
    high = jnp.where(mine, dot(spread, high, NT), 0.0).astype(BF16)
    low = jnp.where(mine, dot(spread, low, NT), 0.0).astype(BF16)
    ones = jnp.ones((cap, table_rows), BF16)
    row_of = dot(high, ones) + dot(low, ones)
    row = lax.broadcasted_iota(jnp.int32, (slots, table_rows), 1).astype(F32)
    pick = as_bf16(row_of == row)
    loads[2].wait()
    fetched = dot(pick, table[...].astype(BF16)).astype(BF16)
    cold_out[...] = fetched.reshape(n_w, cap, depth)

    def send_cold(k):
        wide_part(cold_out, cold_keys, 0, k)

    send_cold(0)
    query_t[...] = jnp.transpose(line_q[0])

    def fold(s, first=False):
        s3 = s.reshape(s.shape[0] // 8, 8, s.shape[1])
        top = jnp.max(s3, axis=0)
        if first:
            top8[...] = top
            sum8[...] = jnp.sum(jnp.exp(s3 - top[None]), axis=0)
        else:
            before = top8[...]
            top = jnp.maximum(before, top)
            top8[...] = top
            sum8[...] = sum8[...] * jnp.exp(before - top) + jnp.sum(jnp.exp(s3 - top[None]), axis=0)

    def score(block, first=False):
        s = dot(keys[block], query_t[...]) * scale
        s_in[block] = s
        fold(s, first)

    def score_cold(k):
        at = pl.ds(k * cold_rows, cold_rows)
        owner = lax.broadcasted_iota(jnp.int32, (cold_rows, n_w), 1)
        slot = lax.broadcasted_iota(jnp.int32, (cold_rows, n_w), 0) + k * cold_rows
        spread = as_bf16(lax.div(slot, cap) == owner)
        counts = jnp.broadcast_to(live_counts[...].astype(F32).astype(BF16), (rows, n_w))
        counts = dot(spread, counts, NT)
        place = lax.rem(lax.broadcasted_iota(jnp.int32, (cold_rows, rows), 0), cap).astype(F32)
        owners = pl.ds(k * (n_w // cold_blocks), n_w // cold_blocks)
        found = cold_keys[owners].reshape(cold_rows, depth)
        s = dot(found, query_t[...]) * scale
        s = jnp.where(place < counts, s, -jnp.inf)
        s_cold[at] = s
        fold(s)


    score(0, first=True)

    def score_query(step):
        for block in {step, n_g - step} if isinstance(step, int) else (step, n_g - step):
            s_back[block] = dot(keys[0], line_q[block], NT) * scale

    looped = max(half - 2, 0)
    cold_first = half - 1 - (cold_blocks + 1) // 2
    in_loop = looped >= cold_blocks and cold_first > (cold_blocks + 1) // 2

    if not in_loop:
        for k in range(1, cold_blocks):
            send_cold(k)

    def items_work(n):
        for part in (0, 1):
            if in_loop and not isinstance(n, int):
                k = 2 * (n - 1) + part + 1

                @pl.when(k < cold_blocks)
                def _():
                    send_cold(k)

                if part == 0:

                    @pl.when(n == cold_first)
                    def _():
                        wide_arrived(cold_keys, 0)

                k = 2 * (n - cold_first) + part

                @pl.when((k >= 0) & (k < cold_blocks))
                def _():
                    score_cold(k)

        score(n)
        if not isinstance(n, int) or n < half:
            score(n_g - n)

    def passed_by(n):
        return PARTS * n * RATE[0] // RATE[1]

    @pl.loop(1, half - 1)
    def _(n):
        for part in range(PARTS):
            advance(0, n, part)

        @pl.loop(passed_by(n - 1), passed_by(n))
        def _(e):
            advance(1, e // PARTS + 1, lax.rem(e, PARTS))

        items_work(n)

        @pl.when(passed_by(n) // PARTS > passed_by(n - 1) // PARTS)
        def _():
            score_query(passed_by(n) // PARTS)

    if not in_loop:
        wide_arrived(cold_keys, 0)
        for k in range(cold_blocks):
            score_cold(k)

    events = [(m, part) for m in range(1, half + 1) for part in range(PARTS)]
    queue = events[passed_by(looped) :]
    passed = events[: passed_by(looped)]

    def query_step():
        if queue:
            step, part = queue.pop(0)
            advance(1, step, part)
            passed.append((step, part))
            if part == PARTS - 1:
                score_query(step)

    for n in range(looped + 1, half + 1):
        for part in range(PARTS):
            advance(0, n, part)
        items_work(n)
        for _ in range(passed_by(n) - passed_by(n - 1)):
            query_step()

    top = jnp.max(top8[...], axis=0, keepdims=True)
    total = jnp.sum(sum8[...] * jnp.exp(top8[...] - top), axis=0, keepdims=True)
    lse_all[0] = top + jnp.log(total)

    def lse_copy(p):
        return pltpu.make_async_remote_copy(
            src_ref=lse_all.at[0],
            dst_ref=lse_all.at[p],
            send_sem=lse_send.at[p],
            recv_sem=lse_recv.at[p],
            device_id=(w, lax.rem(g + p, n_g)),
            device_id_type=MESH,
        )

    @pl.loop(1, n_g)
    def _(p):
        lse_copy(p).start()

    @pl.loop(0, cold_blocks)
    def _(k):
        d = jnp.exp(s_cold[pl.ds(k * cold_rows, cold_rows)] - lse_all[0]).astype(BF16)
        back = (dot(d, line_q[0]) * scale).astype(BF16)
        slot_out[pl.ds(k * per, per)] = back.reshape(per, cap, depth)

    for i in range(cold_blocks):
        wide_part(slot_out, slot_back, 1, i)
        for _ in range(max(PARTS // 4, 1)):
            query_step()

    d = jnp.exp(s_in[0] - lse_all[0])
    key = lax.broadcasted_iota(jnp.int32, d.shape, 0)
    query = lax.broadcasted_iota(jnp.int32, d.shape, 1)
    d = (d - jnp.where(key == query, 1.0, 0.0)).astype(BF16)
    query_grad[...] = dot(d, keys[0], TN)
    item_grad[...] = dot(d, line_q[0])

    jobs = n_g - 1 + cold_blocks

    def to_queries(i):
        @pl.when(i < n_g - 1)
        def _():
            d = jnp.exp(s_in[1 + i] - lse_all[0]).astype(BF16)
            query_grad[...] += dot(d, keys[1 + i], TN)

        @pl.when((i >= n_g - 1) & (i < jobs))
        def _():
            k = i - (n_g - 1)
            d = jnp.exp(s_cold[pl.ds(k * cold_rows, cold_rows)] - lse_all[0]).astype(BF16)
            found = cold_keys[pl.ds(k * per, per)].reshape(cold_rows, depth)
            query_grad[...] += dot(d, found, TN)

    def to_items(block):
        d = jnp.exp(s_back[block] - lse_all[block]).astype(BF16)
        item_grad[...] += dot(d, line_q[block])

    owner = lax.broadcasted_iota(jnp.int32, (n_w, slots), 0)
    slot = lax.broadcasted_iota(jnp.int32, (n_w, slots), 1)
    spread = as_bf16(lax.div(slot, cap) == owner)
    picks = send_rows[...]
    high = dot((picks & ~15).astype(F32).astype(BF16), spread)
    low = dot((picks & 15).astype(F32).astype(BF16), spread)
    place = lax.broadcasted_iota(jnp.int32, (cap, slots), 0)
    slot = lax.broadcasted_iota(jnp.int32, (cap, slots), 1)
    row_of = jnp.sum(
        jnp.where(lax.rem(slot, cap) == place, high + low, 0.0), axis=0, keepdims=True
    )
    row = lax.broadcasted_iota(jnp.int32, (table_rows, slots), 0).astype(F32)
    put[...] = as_bf16(row_of == row)

    @pl.loop(1, n_g)
    def _(p):
        lse_copy(p).wait_recv()

    whole = min(len(passed) // PARTS, half - 1)
    ready = [(step, n_g - step) for step in range(1, whole + 1)]
    turns = max(len(queue) - PARTS // 2, 0)
    for turn in range(turns):

        @pl.loop(jobs * turn // turns, jobs * (turn + 1) // turns)
        def _(i):
            to_queries(i)

        query_step()
        if ready and 2 * turn >= turns * (whole - len(ready)) // max(whole, 1):
            for block in ready.pop(0):
                to_items(block)
        step, part = passed[-1]
        if part == PARTS - 1 and step < half:
            ready.append((step, n_g - step))

    if turns == 0:

        @pl.loop(0, jobs)
        def _(i):
            to_queries(i)

    for blocks in ready:
        for block in blocks:
            to_items(block)

    query_grad[...] = query_grad[...] * scale

    def update():
        wide_arrived(slot_back, 1)
        loads[3].wait()
        grad = dot(put[...], slot_back[...].reshape(slots, depth))
        new_table[...] = table[...] - 0.5 * grad / jnp.sqrt(accum[...] + grad * grad)

    update()
    while queue:
        query_step()
        step, part = passed[-1]
        if part == PARTS - 1 and step < half:
            to_items(step)
            to_items(n_g - step)
    to_items(half)
    item_grad[...] = item_grad[...] * scale

    wide_drain(cold_out, 0)
    wide_drain(slot_out, 1)

    @pl.loop(1, n_g)
    def _(p):
        lse_copy(p).wait_send()

    for way in (0, 1):
        for part in range(PARTS):
            for line in (0, 1):

                @pl.loop(1, steps_of(line, way, part) + 1)
                def _(n):
                    ring(line, way, part, n).wait_send()


def store(*refs):
    sems = refs[-1]
    copies = [pltpu.make_async_copy(refs[i], refs[3 + i], sems.at[i]) for i in range(3)]
    for copy in copies:
        copy.start()
    for copy in copies:
        copy.wait()


def on_device(n_w, n_g, queries, items, cold_table, accum, send_rows, live_counts):
    rows, depth = queries.shape
    table_rows = cold_table.shape[0]
    cap = send_rows.shape[1]
    slots = n_w * cap
    half = n_g // 2
    vmem = pl.BlockSpec(memory_space=pltpu.VMEM)
    hbm = pl.BlockSpec(memory_space=pl.ANY)
    limit = 60 * 1024 * 1024
    ring_sems = pltpu.SemaphoreType.DMA((2, 2, PARTS, half + 1))
    results = pl.pallas_call(
        functools.partial(kernel, n_w, n_g, cap),
        out_shape=(
            pltpu.VMEM((rows, depth), F32),
            pltpu.VMEM((rows, depth), F32),
            pltpu.VMEM((table_rows, depth), F32),
        ),
        in_specs=[hbm, hbm, hbm, hbm, vmem, vmem],
        out_specs=(vmem, vmem, vmem),
        scratch_shapes=[
            pltpu.VMEM((n_g, rows, depth), BF16),
            pltpu.VMEM((n_g, rows, depth), BF16),
            pltpu.VMEM((n_g, 1, rows), F32),
            pltpu.VMEM((n_g, rows, rows), F32),
            pltpu.VMEM((n_g, rows, rows), F32),
            pltpu.VMEM((slots, rows), F32),
            pltpu.VMEM((8, rows), F32),
            pltpu.VMEM((8, rows), F32),
            pltpu.VMEM((table_rows, depth), F32),
            pltpu.VMEM((table_rows, depth), F32),
            pltpu.VMEM((n_w, cap, depth), BF16),
            pltpu.VMEM((n_w, cap, depth), BF16),
            pltpu.VMEM((n_w, cap, depth), BF16),
            pltpu.VMEM((n_w, cap, depth), BF16),
            pltpu.VMEM((depth, rows), BF16),
            pltpu.VMEM((table_rows, slots), BF16),
            pltpu.SemaphoreType.DMA((4,)),
            ring_sems,
            ring_sems,
            pltpu.SemaphoreType.DMA((n_g,)),
            pltpu.SemaphoreType.DMA((n_g,)),
            pltpu.SemaphoreType.DMA((2,)),
            pltpu.SemaphoreType.DMA((2,)),
        ],
        compiler_params=pltpu.CompilerParams(
            collective_id=0, has_side_effects=True, vmem_limit_bytes=limit
        ),
    )(queries, items, cold_table, accum, send_rows.T, live_counts)
    return pl.pallas_call(
        store,
        out_shape=tuple(jax.ShapeDtypeStruct(r.shape, r.dtype) for r in results),
        in_specs=[hbm] * 3,
        out_specs=(hbm,) * 3,
        scratch_shapes=[pltpu.SemaphoreType.DMA((3,))],
        compiler_params=pltpu.CompilerParams(vmem_limit_bytes=4 * 1024 * 1024),
    )(*results)


def solution(mesh):
    spec = P(("wide", "group"), None)
    return jax.shard_map(
        functools.partial(on_device, mesh.shape["wide"], mesh.shape["group"]),
        mesh=mesh,
        in_specs=(spec,) * 6,
        out_specs=(spec,) * 3,
        check_vma=False,
    )
```
